256 devices in a mesh: rep: 16 (over x, y_lo, core), fsdp: 16 (over y_hi, z).
Axes of the slice: x: 4, y: 4 (y_hi: 2, y_lo: 2; y = y_hi * 2 + y_lo), z: 8, core: 2. Of those that a mesh axis runs over, the one named last changes fastest.
Arguments:
- local_params: bfloat16 [16, 256, 28672], P('rep', 'fsdp'), may hold values from -6 to 6
- base_params: float32 [256, 28672], P('fsdp'), may hold values from -6 to 6
- error_buffer: float32 [16, 256, 28672], P('rep', 'fsdp'), may hold values from -4 to 4
- momentum: float32 [256, 28672], P('fsdp'), may hold values from -3 to 3
Outputs:
- new_base: float32 [256, 28672], P('fsdp')
- new_error: float32 [16, 256, 28672], P('rep', 'fsdp')
- new_momentum: float32 [256, 28672], P('fsdp')
The draws below stay inside these ranges and needn't reach their ends.
All inputs are finite; a program needn't handle non-finite values.
Results may differ from the reference program's by a relative error of at most 0.0003.
Values sent between devices are 32-bit elements; how exact they have to be, the bound alone decides.
No kernel may reach another device: no remote copies, remote signals or barrier semaphores. Data moves between devices by JAX's collectives and lax.ppermute only.
A program may use at most 64 MiB of HBM per device.

```python
import math
import jax
import jax.numpy as jnp
from jax import lax

FF = 28672
TILE = 64
BAND = 16
ROWS = 256
N_REP = 16


def block_levels(key, extent, split, low, largest):
    gain, own = 1.0, jax.random.fold_in(key, 6)
    for dim, blocks in split:
        steps = jnp.exp(jax.random.uniform(jax.random.fold_in(own, dim), (blocks,), jnp.float32, low / len(split), largest / len(split)))
        gain = gain * jnp.repeat(steps, extent[dim] // blocks).reshape([-1 if axis == dim else 1 for axis in range(len(extent))])
    return gain


def normal_values(rng, extent, width, bound, shards=(), held_as=jnp.bfloat16):
    level = block_levels(rng, extent, shards, -0.22, 0.18) if shards else 1.0
    array = jax.random.normal(rng, extent, jnp.float32) * width * level
    return jnp.minimum(jnp.maximum(array, -bound), bound).astype(held_as)


def setup_inputs(seed: int = 0) -> dict:
    streams_of = jax.random.split(jax.random.key(seed), 5)
    local_params = normal_values(streams_of[0], (N_REP, ROWS, FF), 1.0, 6.0, ((0, 16), (1, 16)))
    base_params = normal_values(streams_of[1], (ROWS, FF), 1.0, 6.0, ((0, 16),), jnp.float32)
    error_buffer = normal_values(streams_of[2], (N_REP, ROWS, FF), 0.5, 4.0, ((0, 16), (1, 16)), jnp.float32)
    momentum = normal_values(streams_of[3], (ROWS, FF), 0.3, 3.0, ((0, 16),), jnp.float32)
    return {"local_params": local_params, "base_params": base_params, "error_buffer": error_buffer, "momentum": momentum}


outer_rate = 0.7
outer_beta = 0.9

def band_table():
    freq = jnp.arange(BAND, dtype=jnp.float32)[:, None]
    sample = jnp.arange(TILE, dtype=jnp.float32)[None, :]
    scale = jnp.where(freq == 0, math.sqrt(1.0 / TILE), math.sqrt(2.0 / TILE))
    return scale * jnp.cos(math.pi * (2.0 * sample + 1.0) * freq / (2.0 * TILE))

def forward_band(field, lowband):
    tiles = field.reshape(ROWS // TILE, TILE, FF // TILE, TILE)
    return jnp.einsum('ka,iajb,lb->ikjl', lowband, tiles, lowband, precision=lax.Precision.HIGHEST)

def inverse_band(coeffs, lowband):
    tiles = jnp.einsum('ka,ikjl,lb->iajb', lowband, coeffs, lowband, precision=lax.Precision.HIGHEST)
    return tiles.reshape(ROWS, FF)

def reference(local_params, base_params, error_buffer, momentum):
    lowband = band_table()

    def one_replica(pair):
        local_one, error_one = pair
        pseudo_grad = base_params - local_one.astype(jnp.float32) + error_one
        coeffs = forward_band(pseudo_grad, lowband)
        return (coeffs, pseudo_grad - inverse_band(coeffs, lowband))
    coefficients, new_error = lax.map(one_replica, (local_params, error_buffer))
    mean_coeff = lax.optimization_barrier(jnp.sum(coefficients, axis=0)) / N_REP
    outer_grad = inverse_band(mean_coeff, lowband)
    new_momentum = outer_beta * momentum + outer_grad
    new_base = base_params - outer_rate * (outer_grad + outer_beta * new_momentum)
    return (new_base, new_error, new_momentum)
```

```python
import functools
import math

import jax
import jax.numpy as jnp
import ml_dtypes
import numpy as np
from jax import lax
from jax.experimental import pallas as pl
from jax.experimental.pallas import tpu as pltpu
from jax.sharding import PartitionSpec as P

TILE = 64
BAND = 16
OUTER_RATE = 0.7
OUTER_BETA = 0.9

PARTS = 4
ROWS = TILE // PARTS
GROUP_TILES = 8
GROUP = GROUP_TILES * TILE
WIDE = GROUP_TILES * BAND
VMEM_LIMIT = 40 * 1024 * 1024

HBM = pl.BlockSpec(memory_space=pltpu.HBM)
VMEM = pl.BlockSpec(memory_space=pltpu.VMEM)


def split_np(table):
    high = table.astype(np.float32).astype(ml_dtypes.bfloat16)
    low = (table - high.astype(np.float64)).astype(np.float32).astype(ml_dtypes.bfloat16)
    return high, low


def tables():
    freq = np.arange(BAND, dtype=np.float64)[:, None]
    sample = np.arange(TILE, dtype=np.float64)[None, :]
    scale = np.where(freq == 0, math.sqrt(1.0 / TILE), math.sqrt(2.0 / TILE))
    lowband = scale * np.cos(math.pi * (2.0 * sample + 1.0) * freq / (2.0 * TILE))
    high, low = split_np(np.kron(np.eye(GROUP_TILES), lowband.T))
    col_fwd = np.concatenate([high, low], axis=1)
    col_inv = np.stack([np.concatenate([t.T, t.T], axis=0) for t in (high, low)])
    blocks = [lowband[:, ROWS * part : ROWS * (part + 1)] for part in range(PARTS)]
    rows_fwd = np.stack(blocks).astype(np.float32)
    rows_inv = np.stack([b.T for b in blocks]).astype(np.float32)
    return col_fwd, col_inv, rows_fwd, rows_inv


def split(value):
    high = value.astype(jnp.bfloat16)
    low = (value - high.astype(jnp.float32)).astype(jnp.bfloat16)
    return high, low


def dot(a, b):
    return jnp.dot(a, b, preferred_element_type=jnp.float32)


def apply_rows(table, value):
    deep = value.reshape(-1, table.shape[1], value.shape[1])
    total = None
    for a in range(table.shape[1]):
        term = table[None, :, a : a + 1] * deep[:, a : a + 1, :]
        total = term if total is None else total + term
    return total.reshape(-1, value.shape[1])


def position():
    part = lax.axis_index("fsdp") % PARTS
    core = lax.axis_index("rep") % 2
    return part, core


def quarter_cols(part, s, width):
    size = width // PARTS
    return pl.ds(pl.multiple_of((part ^ s) * size, GROUP), size)


def forward_kernel(base, local, err, col, rows, out, base_v, local_v, err_v, sems):
    part, core = position()
    width = base.shape[1]
    copies = []
    for s in range(PARTS):
        cols = quarter_cols(part, s, width)
        copies.append(
            [
                pltpu.make_async_copy(base.at[:, cols], base_v.at[s], sems.at[s, 0]),
                pltpu.make_async_copy(err.at[0, :, cols], err_v.at[s], sems.at[s, 1]),
                pltpu.make_async_copy(local.at[0, :, cols], local_v.at[s], sems.at[s, 2]),
            ]
        )
    for step in copies:
        for copy in step:
            copy.start()
    table = rows[part]
    for s in range(PARTS):
        for copy in copies[s]:
            copy.wait()
        field = base_v[s] - local_v[s].astype(jnp.float32) + err_v[s]
        groups = field.shape[1] // GROUP
        stacked = jnp.concatenate([field[:, GROUP * g : GROUP * (g + 1)] for g in range(groups)], axis=0)
        count = stacked.shape[0]
        both = dot(jnp.concatenate(split(stacked), axis=0), col[...])
        both = both[:, :WIDE] + both[:, WIDE:]
        coeffs = apply_rows(table, both[:count] + both[count:])
        half = count // 2
        out[s, core] = coeffs[:half]
        out[s, 1 - core] = coeffs[half:]


def inverse_rows(table, col, coeffs):
    both = jnp.concatenate(split(apply_rows(table, coeffs)), axis=1)
    return dot(both, col[0]) + dot(both, col[1])


def error_kernel(k0, k1, k2, k3, base, local, err, col, rows, out, base_v, local_v, err_v, out_v, sems):
    part, core = position()
    width = base.shape[1]
    copies, writes = [], []
    for s in range(PARTS):
        cols = quarter_cols(part, s, width)
        copies.append(
            [
                pltpu.make_async_copy(base.at[:, cols], base_v.at[s], sems.at[s, 0]),
                pltpu.make_async_copy(err.at[0, :, cols], err_v.at[s], sems.at[s, 1]),
                pltpu.make_async_copy(local.at[0, :, cols], local_v.at[s], sems.at[s, 2]),
            ]
        )
        writes.append(pltpu.make_async_copy(out_v.at[s], out.at[0, :, cols], sems.at[s, 3]))
    for step in copies:
        for copy in step:
            copy.start()
    table = rows[part]
    for s, k in enumerate((k0, k1, k2, k3)):
        coeffs = jnp.concatenate([k[core], k[1 - core]], axis=0)
        kept = inverse_rows(table, col, coeffs)
        for copy in copies[s]:
            copy.wait()
        for g in range(coeffs.shape[0] // ROWS):
            at = slice(GROUP * g, GROUP * (g + 1))
            field = base_v[s, :, at] - local_v[s, :, at].astype(jnp.float32) + err_v[s, :, at]
            out_v[s, :, at] = field - kept[ROWS * g : ROWS * (g + 1)]
        writes[s].start()
    for write in writes:
        write.wait()


def update_kernel(replicas, own, other, base, mom, col, rows, base_out, mom_out, base_w, mom_w, sems):
    part, core = position()
    width = base.shape[1]
    table = rows[part]
    writes = []
    for s in range(PARTS):
        cols = quarter_cols(part, s, width)
        both = jnp.stack([own[s], other[s]]) * (1.0 / replicas)
        first = jnp.where(core == 0, both[0], both[1])
        second = jnp.where(core == 0, both[1], both[0])
        outer = inverse_rows(table, col, jnp.concatenate([first, second], axis=0))
        size = width // PARTS
        for g in range(size // GROUP):
            at = slice(GROUP * g, GROUP * (g + 1))
            src = pl.ds(pl.multiple_of((part ^ s) * size + GROUP * g, GROUP), GROUP)
            grad = outer[ROWS * g : ROWS * (g + 1)]
            new_momentum = OUTER_BETA * mom[:, src] + grad
            mom_w[s, :, at] = new_momentum
            base_w[s, :, at] = base[:, src] - OUTER_RATE * (grad + OUTER_BETA * new_momentum)
        for i, (src, dst) in enumerate(((base_w, base_out), (mom_w, mom_out))):
            writes.append(pltpu.make_async_copy(src.at[s], dst.at[:, cols], sems.at[s, i]))
            writes[-1].start()
    for write in writes:
        write.wait()


def call(kernel, name, inputs, in_specs, out_specs, out_shape, scratch, flops, moved):
    return pl.pallas_call(
        kernel,
        in_specs=in_specs,
        out_specs=out_specs,
        out_shape=out_shape,
        scratch_shapes=scratch,
        compiler_params=pltpu.CompilerParams(vmem_limit_bytes=VMEM_LIMIT),
        cost_estimate=pl.CostEstimate(flops=flops, bytes_accessed=moved, transcendentals=0),
        name=name,
    )(*inputs)


def in_hbm(value):
    return pltpu.with_memory_space_constraint(value, pltpu.HBM)


def local(local_params, base_params, error_buffer, momentum):
    rows, width = base_params.shape
    replicas = lax.axis_size("rep")
    shards = lax.axis_size("fsdp")
    quarter_rows = width // PARTS // GROUP * ROWS
    col_fwd, col_inv, rows_fwd, rows_inv = (jnp.asarray(t) for t in tables())
    f32 = lambda *shape: jax.ShapeDtypeStruct(shape, jnp.float32)
    buffer = lambda dtype=jnp.float32: pltpu.VMEM((PARTS, rows, width // PARTS), dtype)
    cells = rows * width

    partial = call(
        forward_kernel, "forward",
        (in_hbm(base_params), in_hbm(local_params), in_hbm(error_buffer), col_fwd, rows_fwd),
        [HBM, HBM, HBM, VMEM, VMEM],
        VMEM, pltpu.VMEM((PARTS, 2, quarter_rows // 2, WIDE), jnp.float32),
        [buffer(), buffer(jnp.bfloat16), buffer(), pltpu.SemaphoreType.DMA((PARTS, 3))],
        flops=cells * 1024, moved=cells * 11,
    )

    def along_z(value, s):
        return lax.ppermute(value, "fsdp", [(i, i ^ s) for i in range(shards)])

    def along_rep(value, s):
        return lax.ppermute(value, "rep", [(i, i ^ s) for i in range(replicas)])

    quarter = partial[0] + along_z(partial[1], 1) + along_z(partial[2], 2) + along_z(partial[3], 3)
    next1, next2 = along_z(quarter, 1), along_z(quarter, 2)
    next3 = along_z(next2, 1)
    total = quarter[0] + along_rep(quarter[1], 1)
    total = total + along_rep(total, 2)
    total = total + along_rep(total, 4) + along_rep(total, 8) + along_rep(total, 12)
    next1, next2, next3, total = lax.optimization_barrier((next1, next2, next3, total))
    own_pieces = [total] + [along_z(total, s) for s in range(1, PARTS)]

    new_error = call(
        error_kernel, "error",
        (quarter, next1, next2, next3, in_hbm(base_params), in_hbm(local_params), in_hbm(error_buffer), col_inv, rows_inv),
        [VMEM] * PARTS + [HBM, HBM, HBM, VMEM, VMEM],
        HBM, f32(1, rows, width),
        [buffer(), buffer(jnp.bfloat16), buffer(), buffer(), pltpu.SemaphoreType.DMA((PARTS, 4))],
        flops=cells * 1024, moved=cells * 15,
    )
    *own_pieces, new_error = lax.optimization_barrier((*own_pieces, new_error))
    own = jnp.stack(own_pieces)
    other = along_rep(own, 1)
    new_base, new_momentum = call(
        functools.partial(update_kernel, replicas), "update",
        (own, other, base_params, momentum, col_inv, rows_inv),
        [VMEM] * 6,
        [HBM, HBM], [f32(rows, width), f32(rows, width)],
        [buffer(), buffer(), pltpu.SemaphoreType.DMA((PARTS, 2))],
        flops=cells * 1024, moved=cells * 16,
    )
    return (new_base, new_error, new_momentum)


def solution(mesh):
    in_specs = (P("rep", "fsdp", None), P("fsdp", None), P("rep", "fsdp", None), P("fsdp", None))
    out_specs = (P("fsdp", None), P("rep", "fsdp", None), P("fsdp", None))
    return jax.shard_map(local, mesh=mesh, in_specs=in_specs, out_specs=out_specs, check_vma=False)
```

```python
import functools
import math

import jax
import jax.numpy as jnp
import ml_dtypes
import numpy as np
from jax import lax
from jax.experimental import pallas as pl
from jax.experimental.pallas import tpu as pltpu
from jax.sharding import PartitionSpec as P

TILE = 64
BAND = 16
OUTER_RATE = 0.7
OUTER_BETA = 0.9

PARTS = 4
ROWS = TILE // PARTS
GROUP_TILES = 8
GROUP = GROUP_TILES * TILE
WIDE = GROUP_TILES * BAND
VMEM_LIMIT = 40 * 1024 * 1024

HBM = pl.BlockSpec(memory_space=pltpu.HBM)
VMEM = pl.BlockSpec(memory_space=pltpu.VMEM)


def split_np(table):
    high = table.astype(np.float32).astype(ml_dtypes.bfloat16)
    low = (table - high.astype(np.float64)).astype(np.float32).astype(ml_dtypes.bfloat16)
    return high, low


def tables():
    freq = np.arange(BAND, dtype=np.float64)[:, None]
    sample = np.arange(TILE, dtype=np.float64)[None, :]
    scale = np.where(freq == 0, math.sqrt(1.0 / TILE), math.sqrt(2.0 / TILE))
    lowband = scale * np.cos(math.pi * (2.0 * sample + 1.0) * freq / (2.0 * TILE))
    high, low = split_np(np.kron(np.eye(GROUP_TILES), lowband.T))
    col_fwd = np.concatenate([high, low], axis=1)
    col_inv = np.stack([np.concatenate([t.T, t.T], axis=0) for t in (high, low)])
    blocks = [lowband[:, ROWS * part : ROWS * (part + 1)] for part in range(PARTS)]
    rows_fwd = np.stack(blocks).astype(np.float32)
    rows_inv = np.stack([b.T for b in blocks]).astype(np.float32)
    return col_fwd, col_inv, rows_fwd, rows_inv


def split(value):
    high = value.astype(jnp.bfloat16)
    low = (value - high.astype(jnp.float32)).astype(jnp.bfloat16)
    return high, low


def dot(a, b):
    return jnp.dot(a, b, preferred_element_type=jnp.float32)


def apply_rows(table, value):
    deep = value.reshape(-1, table.shape[1], value.shape[1])
    total = None
    for a in range(table.shape[1]):
        term = table[None, :, a : a + 1] * deep[:, a : a + 1, :]
        total = term if total is None else total + term
    return total.reshape(-1, value.shape[1])


def position():
    part = lax.axis_index("fsdp") % PARTS
    core = lax.axis_index("rep") % 2
    return part, core


def quarter_cols(part, s, width):
    size = width // PARTS
    return pl.ds(pl.multiple_of((part ^ s) * size, GROUP), size)


def forward_kernel(steps, base, local, err, col, rows, out, base_v, local_v, err_v, col_v, rows_v, sems, table_sems):
    part, core = position()
    width = base.shape[1]
    tables = (
        pltpu.make_async_copy(col, col_v, table_sems.at[0]),
        pltpu.make_async_copy(rows.at[part], rows_v, table_sems.at[1]),
    )
    copies = []
    for i, s in enumerate(steps):
        cols = quarter_cols(part, s, width)
        copies.append(
            [
                pltpu.make_async_copy(base.at[:, cols], base_v.at[i], sems.at[i, 0]),
                pltpu.make_async_copy(err.at[0, :, cols], err_v.at[i], sems.at[i, 1]),
                pltpu.make_async_copy(local.at[0, :, cols], local_v.at[i], sems.at[i, 2]),
            ]
        )
    for copy in (*copies[0], *tables, *(copy for step in copies[1:] for copy in step)):
        copy.start()
    for i in range(len(steps)):
        for copy in copies[i]:
            copy.wait()
        if i == 0:
            for copy in tables:
                copy.wait()
        field = base_v[i] - local_v[i].astype(jnp.float32) + err_v[i]
        groups = field.shape[1] // GROUP
        stacked = jnp.concatenate([field[:, GROUP * g : GROUP * (g + 1)] for g in range(groups)], axis=0)
        count = stacked.shape[0]
        both = dot(jnp.concatenate(split(stacked), axis=0), col_v[...])
        both = both[:, :WIDE] + both[:, WIDE:]
        coeffs = apply_rows(rows_v[...], both[:count] + both[count:])
        half = count // 2
        out[i, core] = coeffs[:half]
        out[i, 1 - core] = coeffs[half:]


def inverse_rows(table, col, coeffs):
    both = jnp.concatenate(split(apply_rows(table, coeffs)), axis=1)
    return dot(both, col[0]) + dot(both, col[1])


def error_kernel(k0, k1, k2, k3, base, local, err, col, rows, out, base_v, local_v, err_v, out_v, sems):
    part, core = position()
    width = base.shape[1]
    copies, writes = [], []
    for s in range(PARTS):
        cols = quarter_cols(part, s, width)
        copies.append(
            [
                pltpu.make_async_copy(base.at[:, cols], base_v.at[s], sems.at[s, 0]),
                pltpu.make_async_copy(err.at[0, :, cols], err_v.at[s], sems.at[s, 1]),
                pltpu.make_async_copy(local.at[0, :, cols], local_v.at[s], sems.at[s, 2]),
            ]
        )
        writes.append(pltpu.make_async_copy(out_v.at[s], out.at[0, :, cols], sems.at[s, 3]))
    for step in copies:
        for copy in step:
            copy.start()
    table = rows[part]
    for s, k in enumerate((k0, k1, k2, k3)):
        coeffs = jnp.concatenate([k[core], k[1 - core]], axis=0)
        kept = inverse_rows(table, col, coeffs)
        for copy in copies[s]:
            copy.wait()
        for g in range(coeffs.shape[0] // ROWS):
            at = slice(GROUP * g, GROUP * (g + 1))
            field = base_v[s, :, at] - local_v[s, :, at].astype(jnp.float32) + err_v[s, :, at]
            out_v[s, :, at] = field - kept[ROWS * g : ROWS * (g + 1)]
        writes[s].start()
    for write in writes:
        write.wait()


def update_kernel(replicas, half, mean, base, mom, col, rows, *refs):
    base_out, mom_out, base_w, mom_w, sems = refs[-5:]
    part, core = position()
    width = base.shape[1]
    table = rows[part]
    size = width // PARTS // 2
    here = core if half == 0 else 1 - core
    writes = []
    for s in range(PARTS):
        start = ((part ^ s) * 2 + here) * size
        outer = inverse_rows(table, col, mean[s] * (1.0 / replicas))
        for g in range(size // GROUP):
            at = slice(GROUP * g, GROUP * (g + 1))
            src = pl.ds(pl.multiple_of(start + GROUP * g, GROUP), GROUP)
            grad = outer[ROWS * g : ROWS * (g + 1)]
            new_momentum = OUTER_BETA * mom[:, src] + grad
            mom_w[s, :, at] = new_momentum
            base_w[s, :, at] = base[:, src] - OUTER_RATE * (grad + OUTER_BETA * new_momentum)
        cols = pl.ds(pl.multiple_of(start, GROUP), size)
        for i, (src, dst) in enumerate(((base_w, base_out), (mom_w, mom_out))):
            writes.append(pltpu.make_async_copy(src.at[s], dst.at[:, cols], sems.at[s, i]))
            writes[-1].start()
    for write in writes:
        write.wait()


def call(kernel, name, inputs, in_specs, out_specs, out_shape, scratch, flops, moved, aliases={}):
    return pl.pallas_call(
        kernel,
        in_specs=in_specs,
        out_specs=out_specs,
        out_shape=out_shape,
        scratch_shapes=scratch,
        compiler_params=pltpu.CompilerParams(vmem_limit_bytes=VMEM_LIMIT),
        cost_estimate=pl.CostEstimate(flops=flops, bytes_accessed=moved, transcendentals=0),
        input_output_aliases=aliases,
        name=name,
    )(*inputs)


def in_hbm(value):
    return pltpu.with_memory_space_constraint(value, pltpu.HBM)


def local(local_params, base_params, error_buffer, momentum):
    rows, width = base_params.shape
    replicas = lax.axis_size("rep")
    shards = lax.axis_size("fsdp")
    quarter_rows = width // PARTS // GROUP * ROWS
    col_fwd, col_inv, rows_fwd, rows_inv = (jnp.asarray(t) for t in tables())
    f32 = lambda *shape: jax.ShapeDtypeStruct(shape, jnp.float32)
    buffer = lambda dtype=jnp.float32: pltpu.VMEM((PARTS, rows, width // PARTS), dtype)
    cells = rows * width

    def forward(*steps):
        count = len(steps)
        pair = lambda dtype=jnp.float32: pltpu.VMEM((count, rows, width // PARTS), dtype)
        coeffs = call(
            functools.partial(forward_kernel, steps), "forward",
            [in_hbm(v) for v in (base_params, local_params, error_buffer, col_fwd, rows_fwd)],
            [HBM] * 5,
            VMEM, pltpu.VMEM((count, 2, quarter_rows // 2, WIDE), jnp.float32),
            [pair(), pair(jnp.bfloat16), pair(), pltpu.VMEM(col_fwd.shape, jnp.bfloat16), pltpu.VMEM(rows_fwd.shape[1:], jnp.float32),
             pltpu.SemaphoreType.DMA((count, 3)), pltpu.SemaphoreType.DMA((2,))],
            flops=cells * 256 * count, moved=cells * 11 * count // PARTS,
        )
        return tuple(coeffs[i] for i in range(count))

    def along_z(value, s, name):
        with jax.named_scope(f"{name}{s}"):
            return lax.ppermute(value, "fsdp", [(i, i ^ s) for i in range(shards)])

    def along_rep(value, s, name):
        with jax.named_scope(f"{name}{s}"):
            return lax.ppermute(value, "rep", [(i, i ^ s) for i in range(replicas)])

    (part2,) = forward(2)
    far2 = along_z(part2, 2, "far")
    part3, part1, part0 = forward(3, 1, 0)
    near1 = along_z(part1, 1, "near")
    far3 = along_z(part3, 3, "far")
    quarter = part0 + near1 + far3 + far2
    total = quarter[0] + along_rep(quarter[1], 1, "core")
    total = total + along_rep(total, 2, "ylo")
    x12, x4, x8 = (along_rep(total, s, "x") for s in (12, 4, 8))
    next1, next3, next2 = (along_z(quarter, s, "next") for s in (1, 3, 2))
    next1, next2, next3, x8 = lax.optimization_barrier((next1, next2, next3, x8))
    total = total + x8 + x4 + x12
    own_pieces = [total] + [along_z(total, s, "mean") for s in range(1, PARTS)]

    new_error = call(
        error_kernel, "error",
        (quarter, next1, next2, next3, in_hbm(base_params), in_hbm(local_params), in_hbm(error_buffer), col_inv, rows_inv),
        [VMEM] * PARTS + [HBM, HBM, HBM, VMEM, VMEM],
        HBM, f32(1, rows, width),
        [buffer(), buffer(jnp.bfloat16), buffer(), buffer(), pltpu.SemaphoreType.DMA((PARTS, 4))],
        flops=cells * 1024, moved=cells * 15,
    )
    *own_pieces, new_error = lax.optimization_barrier((*own_pieces, new_error))
    own = jnp.stack(own_pieces)
    other = along_rep(own, 1, "swap")
    state = ()
    for half, mean in enumerate((own, other)):
        piece = pltpu.VMEM((PARTS, rows, width // PARTS // 2), jnp.float32)
        state = call(
            functools.partial(update_kernel, replicas, half), "update",
            (mean, base_params, momentum, col_inv, rows_inv, *state),
            [VMEM] * 5 + [HBM] * len(state),
            [HBM, HBM], [f32(rows, width), f32(rows, width)],
            [piece, piece, pltpu.SemaphoreType.DMA((PARTS, 2))],
            flops=cells * 512, moved=cells * 8,
            aliases={5 + i: i for i in range(len(state))},
        )
    new_base, new_momentum = state
    return (new_base, new_error, new_momentum)


def solution(mesh):
    in_specs = (P("rep", "fsdp", None), P("fsdp", None), P("rep", "fsdp", None), P("fsdp", None))
    out_specs = (P("fsdp", None), P("rep", "fsdp", None), P("fsdp", None))
    return jax.shard_map(local, mesh=mesh, in_specs=in_specs, out_specs=out_specs, check_vma=False)
```

```python
import functools
import math

import jax
import jax.numpy as jnp
import ml_dtypes
import numpy as np
from jax import lax
from jax.experimental import pallas as pl
from jax.experimental.pallas import tpu as pltpu
from jax.sharding import PartitionSpec as P

TILE = 64
BAND = 16
OUTER_RATE = 0.7
OUTER_BETA = 0.9

PARTS = 4
ROWS = TILE // PARTS
GROUP_TILES = 8
GROUP = GROUP_TILES * TILE
WIDE = GROUP_TILES * BAND
VMEM_LIMIT = 24 * 1024 * 1024

HBM = pl.BlockSpec(memory_space=pltpu.HBM)
VMEM = pl.BlockSpec(memory_space=pltpu.VMEM)


def split_np(table):
    high = table.astype(np.float32).astype(ml_dtypes.bfloat16)
    low = (table - high.astype(np.float64)).astype(np.float32).astype(ml_dtypes.bfloat16)
    return high, low


def tables():
    freq = np.arange(BAND, dtype=np.float64)[:, None]
    sample = np.arange(TILE, dtype=np.float64)[None, :]
    scale = np.where(freq == 0, math.sqrt(1.0 / TILE), math.sqrt(2.0 / TILE))
    lowband = scale * np.cos(math.pi * (2.0 * sample + 1.0) * freq / (2.0 * TILE))
    high, low = split_np(np.kron(np.eye(GROUP_TILES), lowband.T))
    col_fwd = np.concatenate([high, low], axis=1)
    col_inv = np.stack([np.concatenate([t.T, t.T], axis=0) for t in (high, low)])
    blocks = [lowband[:, ROWS * part : ROWS * (part + 1)] for part in range(PARTS)]
    rows_fwd = np.stack(blocks).astype(np.float32)
    rows_inv = np.stack([b.T for b in blocks]).astype(np.float32)
    return col_fwd, col_inv, rows_fwd, rows_inv


def split(value):
    high = value.astype(jnp.bfloat16)
    low = (value - high.astype(jnp.float32)).astype(jnp.bfloat16)
    return high, low


def dot(a, b):
    return jnp.dot(a, b, preferred_element_type=jnp.float32)


def apply_rows(table, value):
    deep = value.reshape(-1, table.shape[1], value.shape[1])
    total = None
    for a in range(table.shape[1]):
        term = table[None, :, a : a + 1] * deep[:, a : a + 1, :]
        total = term if total is None else total + term
    return total.reshape(-1, value.shape[1])


def position():
    part = lax.axis_index("fsdp") % PARTS
    core = lax.axis_index("rep") % 2
    return part, core


def quarter_cols(part, s, width):
    size = width // PARTS
    return pl.ds(pl.multiple_of((part ^ s) * size, GROUP), size)


def forward_kernel(steps, base, local, err, col, rows, out, kept, base_v, local_v, err_v, col_v, rows_v, sems, table_sems):
    part, core = position()
    width = base.shape[1]
    tables = (
        pltpu.make_async_copy(col, col_v, table_sems.at[0]),
        pltpu.make_async_copy(rows.at[part], rows_v, table_sems.at[1]),
    )
    copies = []
    for i, s in enumerate(steps):
        cols = quarter_cols(part, s, width)
        copies.append(
            [
                pltpu.make_async_copy(base.at[:, cols], base_v.at[i], sems.at[i, 0]),
                pltpu.make_async_copy(err.at[0, :, cols], err_v.at[i], sems.at[i, 1]),
                pltpu.make_async_copy(local.at[0, :, cols], local_v.at[i], sems.at[i, 2]),
            ]
        )
    for copy in (*copies[0], *tables, *(copy for step in copies[1:] for copy in step)):
        copy.start()
    for copy in (*tables, *(copy for step in copies for copy in step)):
        copy.wait()
    stacked = []
    for i in range(len(steps)):
        for g in range(base_v.shape[2] // GROUP):
            at = slice(GROUP * g, GROUP * (g + 1))
            field = base_v[i, :, at] - local_v[i, :, at].astype(jnp.float32) + err_v[i, :, at]
            kept[i, :, at] = field
            stacked.append(field)
    stacked = jnp.concatenate(stacked, axis=0)
    count = stacked.shape[0]
    both = dot(jnp.concatenate(split(stacked), axis=0), col_v[...])
    both = both[:, :WIDE] + both[:, WIDE:]
    coeffs = apply_rows(rows_v[...], both[:count] + both[count:])
    half = count // len(steps) // 2
    for i in range(len(steps)):
        out[i, core] = coeffs[2 * i * half : (2 * i + 1) * half]
        out[i, 1 - core] = coeffs[(2 * i + 1) * half : (2 * i + 2) * half]


def inverse_rows(table, col, coeffs):
    both = jnp.concatenate(split(apply_rows(table, coeffs)), axis=1)
    return dot(both, col[0]) + dot(both, col[1])


def error_kernel(k0, k1, k2, k3, field3, fields, col, rows, out, out_v, sems):
    part, core = position()
    width = out.shape[2]
    order = ((k0, fields.at[2]), (k1, fields.at[1]), (k2, fields.at[0]), (k3, field3.at[0]))
    coeffs = jnp.concatenate([k[h] for k, _ in order for h in (core, 1 - core)], axis=0)
    kept = inverse_rows(rows[part], col, coeffs)
    count = coeffs.shape[0] // PARTS
    writes = []
    for s, (_, field) in enumerate(order):
        for g in range(count // ROWS):
            row = s * count + ROWS * g
            at = slice(GROUP * g, GROUP * (g + 1))
            out_v[s, :, at] = field[:, at] - kept[row : row + ROWS]
        writes.append(pltpu.make_async_copy(out_v.at[s], out.at[0, :, quarter_cols(part, s, width)], sems.at[s]))
        writes[-1].start()
    for write in writes:
        write.wait()


def update_kernel(replicas, pieces, base, mom, col, rows, *refs):
    base_out, mom_out, base_w, mom_w, sems = refs[-5:]
    part, core = position()
    width = base.shape[1]
    size = width // PARTS // 2
    table = rows[part]
    writes = []
    for n, (s, half, which, index) in enumerate(pieces):
        outer = inverse_rows(table, col, refs[which][index] * (1.0 / replicas))
        start = ((part ^ s) * 2 + (core if half == 0 else 1 - core)) * size
        for g in range(size // GROUP):
            at = slice(GROUP * g, GROUP * (g + 1))
            src = pl.ds(pl.multiple_of(start + GROUP * g, GROUP), GROUP)
            grad = outer[ROWS * g : ROWS * (g + 1)]
            new_momentum = OUTER_BETA * mom[:, src] + grad
            mom_w[n, :, at] = new_momentum
            base_w[n, :, at] = base[:, src] - OUTER_RATE * (grad + OUTER_BETA * new_momentum)
        cols = pl.ds(pl.multiple_of(start, GROUP), size)
        for i, (src, dst) in enumerate(((base_w, base_out), (mom_w, mom_out))):
            writes.append(pltpu.make_async_copy(src.at[n], dst.at[:, cols], sems.at[n, i]))
            writes[-1].start()
    for write in writes:
        write.wait()


def call(kernel, name, inputs, in_specs, out_specs, out_shape, scratch, flops, moved, aliases={}):
    return pl.pallas_call(
        kernel,
        in_specs=in_specs,
        out_specs=out_specs,
        out_shape=out_shape,
        scratch_shapes=scratch,
        compiler_params=pltpu.CompilerParams(vmem_limit_bytes=VMEM_LIMIT),
        cost_estimate=pl.CostEstimate(flops=flops, bytes_accessed=moved, transcendentals=0),
        input_output_aliases=aliases,
        name=name,
    )(*inputs)


def in_hbm(value):
    return pltpu.with_memory_space_constraint(value, pltpu.HBM)


def local(local_params, base_params, error_buffer, momentum):
    rows, width = base_params.shape
    replicas = lax.axis_size("rep")
    shards = lax.axis_size("fsdp")
    quarter_rows = width // PARTS // GROUP * ROWS
    col_fwd, col_inv, rows_fwd, rows_inv = (jnp.asarray(t) for t in tables())
    f32 = lambda *shape: jax.ShapeDtypeStruct(shape, jnp.float32)
    buffer = lambda dtype=jnp.float32: pltpu.VMEM((PARTS, rows, width // PARTS), dtype)
    cells = rows * width

    def forward(*steps):
        count = len(steps)
        pair = lambda dtype=jnp.float32: pltpu.VMEM((count, rows, width // PARTS), dtype)
        coeffs, field = call(
            functools.partial(forward_kernel, steps), "forward",
            [in_hbm(v) for v in (base_params, local_params, error_buffer, col_fwd, rows_fwd)],
            [HBM] * 5,
            [VMEM, VMEM], [pltpu.VMEM((count, 2, quarter_rows // 2, WIDE), jnp.float32), pair()],
            [pair(), pair(jnp.bfloat16), pair(), pltpu.VMEM(col_fwd.shape, jnp.bfloat16), pltpu.VMEM(rows_fwd.shape[1:], jnp.float32),
             pltpu.SemaphoreType.DMA((count, 3)), pltpu.SemaphoreType.DMA((2,))],
            flops=cells * 256 * count, moved=cells * 11 * count // PARTS,
        )
        return tuple(coeffs[i] for i in range(count)), field

    def along_z(value, s, name):
        with jax.named_scope(f"{name}{s}"):
            return lax.ppermute(value, "fsdp", [(i, i ^ s) for i in range(shards)])

    def along_rep(value, s, name):
        with jax.named_scope(f"{name}{s}"):
            return lax.ppermute(value, "rep", [(i, i ^ s) for i in range(replicas)])

    (part3,), field3 = forward(3)
    passed = along_z(part3, 1, "pass")
    (part2, part1, part0), fields = forward(2, 1, 0)
    passed, part1 = lax.optimization_barrier((passed, part1))
    far2 = along_z(part2 + passed, 2, "far")
    near1 = along_z(part1, 1, "near")
    quarter = part0 + far2 + near1
    total = quarter[0] + along_rep(quarter[1], 1, "core")
    total = total + along_rep(total, 2, "ylo")
    x12, x4, x8 = (along_rep(total, s, "x") for s in (12, 4, 8))
    next1, next3, next2 = (along_z(quarter, s, "next") for s in (1, 3, 2))
    next1, next2, next3, x8 = lax.optimization_barrier((next1, next2, next3, x8))
    total = total + x8 + x4 + x12
    own_pieces = [total] + [along_z(total, s, "mean") for s in range(1, PARTS)]

    new_error = call(
        error_kernel, "error",
        (quarter, next1, next2, next3, field3, fields, col_inv, rows_inv),
        [VMEM] * 8,
        HBM, f32(1, rows, width),
        [buffer(), pltpu.SemaphoreType.DMA((PARTS,))],
        flops=cells * 1024, moved=cells * 8,
    )
    *own_pieces, new_error = lax.optimization_barrier((*own_pieces, new_error))
    own = jnp.stack(own_pieces)
    other = along_rep(own, 1, "swap")
    batches = (
        ((own,), tuple((s, 0, 0, s) for s in range(PARTS))),
        ((other,), tuple((s, 1, 0, s) for s in range(PARTS))),
    )
    state = ()
    for means, pieces in batches:
        count = len(pieces)
        piece = pltpu.VMEM((count, rows, width // PARTS // 2), jnp.float32)
        state = call(
            functools.partial(update_kernel, replicas, pieces), "update",
            (base_params, momentum, col_inv, rows_inv, *means, *state),
            [VMEM] * (4 + len(means)) + [HBM] * len(state),
            [HBM, HBM], [f32(rows, width), f32(rows, width)],
            [piece, piece, pltpu.SemaphoreType.DMA((count, 2))],
            flops=cells * 128 * count, moved=cells * 2 * count,
            aliases={4 + len(means) + i: i for i in range(len(state))},
        )
    new_base, new_momentum = state
    return (new_base, new_error, new_momentum)


def solution(mesh):
    in_specs = (P("rep", "fsdp", None), P("fsdp", None), P("rep", "fsdp", None), P("fsdp", None))
    out_specs = (P("fsdp", None), P("rep", "fsdp", None), P("fsdp", None))
    return jax.shard_map(local, mesh=mesh, in_specs=in_specs, out_specs=out_specs, check_vma=False)
```

```python
import functools
import math

import jax
import jax.numpy as jnp
import ml_dtypes
import numpy as np
from jax import lax
from jax.experimental import pallas as pl
from jax.experimental.pallas import tpu as pltpu
from jax.sharding import PartitionSpec as P

TILE = 64
BAND = 16
OUTER_RATE = 0.7
OUTER_BETA = 0.9

PARTS = 4
ROWS = TILE // PARTS
GROUP_TILES = 8
GROUP = GROUP_TILES * TILE
WIDE = GROUP_TILES * BAND
VMEM_LIMIT = 24 * 1024 * 1024

HBM = pl.BlockSpec(memory_space=pltpu.HBM)
VMEM = pl.BlockSpec(memory_space=pltpu.VMEM)


def split_np(table):
    high = table.astype(np.float32).astype(ml_dtypes.bfloat16)
    low = (table - high.astype(np.float64)).astype(np.float32).astype(ml_dtypes.bfloat16)
    return high, low


def tables():
    freq = np.arange(BAND, dtype=np.float64)[:, None]
    sample = np.arange(TILE, dtype=np.float64)[None, :]
    scale = np.where(freq == 0, math.sqrt(1.0 / TILE), math.sqrt(2.0 / TILE))
    lowband = scale * np.cos(math.pi * (2.0 * sample + 1.0) * freq / (2.0 * TILE))
    high, low = split_np(np.kron(np.eye(GROUP_TILES), lowband.T))
    col_fwd = np.concatenate([high, low], axis=1)
    col_inv = np.stack([np.concatenate([t.T, t.T], axis=0) for t in (high, low)])
    blocks = [lowband[:, ROWS * part : ROWS * (part + 1)] for part in range(PARTS)]
    rows_fwd = np.stack(blocks).astype(np.float32)
    rows_inv = np.stack([b.T for b in blocks]).astype(np.float32)
    return col_fwd, col_inv, rows_fwd, rows_inv


def split(value):
    high = value.astype(jnp.bfloat16)
    low = (value - high.astype(jnp.float32)).astype(jnp.bfloat16)
    return high, low


def dot(a, b):
    return jnp.dot(a, b, preferred_element_type=jnp.float32)


def apply_rows(table, value):
    deep = value.reshape(-1, table.shape[1], value.shape[1])
    total = None
    for a in range(table.shape[1]):
        term = table[None, :, a : a + 1] * deep[:, a : a + 1, :]
        total = term if total is None else total + term
    return total.reshape(-1, value.shape[1])


def position():
    part = lax.axis_index("fsdp") % PARTS
    core = lax.axis_index("rep") % 2
    return part, core


def quarter_cols(part, s, width):
    size = width // PARTS
    return pl.ds(pl.multiple_of((part ^ s) * size, GROUP), size)


def forward_kernel(steps, base, local, err, col, rows, out, kept, base_v, local_v, err_v, col_v, rows_v, sems, table_sems):
    part, core = position()
    width = base.shape[1]
    tables = (
        pltpu.make_async_copy(col, col_v, table_sems.at[0]),
        pltpu.make_async_copy(rows.at[part], rows_v, table_sems.at[1]),
    )
    copies = []
    for i, s in enumerate(steps):
        cols = quarter_cols(part, s, width)
        copies.append(
            [
                pltpu.make_async_copy(base.at[:, cols], base_v.at[i], sems.at[i, 0]),
                pltpu.make_async_copy(err.at[0, :, cols], err_v.at[i], sems.at[i, 1]),
                pltpu.make_async_copy(local.at[0, :, cols], local_v.at[i], sems.at[i, 2]),
            ]
        )
    for copy in (*copies[0], *tables, *(copy for step in copies[1:] for copy in step)):
        copy.start()
    for copy in (*tables, *(copy for step in copies for copy in step)):
        copy.wait()
    stacked = []
    for i in range(len(steps)):
        for g in range(base_v.shape[2] // GROUP):
            at = slice(GROUP * g, GROUP * (g + 1))
            field = base_v[i, :, at] - local_v[i, :, at].astype(jnp.float32) + err_v[i, :, at]
            kept[i, :, at] = field
            stacked.append(field)
    stacked = jnp.concatenate(stacked, axis=0)
    count = stacked.shape[0]
    both = dot(jnp.concatenate(split(stacked), axis=0), col_v[...])
    both = both[:, :WIDE] + both[:, WIDE:]
    coeffs = apply_rows(rows_v[...], both[:count] + both[count:])
    half = count // len(steps) // 2
    for i in range(len(steps)):
        out[i, core] = coeffs[2 * i * half : (2 * i + 1) * half]
        out[i, 1 - core] = coeffs[(2 * i + 1) * half : (2 * i + 2) * half]


def inverse_rows(table, col, coeffs):
    both = jnp.concatenate(split(apply_rows(table, coeffs)), axis=1)
    return dot(both, col[0]) + dot(both, col[1])


def error_kernel(k0, k1, k2, k3, field3, fields, col, rows, out, out_v, sems):
    part, core = position()
    width = out.shape[2]
    order = ((k0, fields.at[2]), (k1, fields.at[1]), (k2, fields.at[0]), (k3, field3.at[0]))
    coeffs = jnp.concatenate([k[h] for k, _ in order for h in (core, 1 - core)], axis=0)
    kept = inverse_rows(rows[part], col, coeffs)
    count = coeffs.shape[0] // PARTS
    writes = []
    for s, (_, field) in enumerate(order):
        for g in range(count // ROWS):
            row = s * count + ROWS * g
            at = slice(GROUP * g, GROUP * (g + 1))
            out_v[s, :, at] = field[:, at] - kept[row : row + ROWS]
        writes.append(pltpu.make_async_copy(out_v.at[s], out.at[0, :, quarter_cols(part, s, width)], sems.at[s]))
        writes[-1].start()
    for write in writes:
        write.wait()


def update_kernel(replicas, pieces, base, mom, col, rows, *refs):
    base_out, mom_out, base_w, mom_w, sems = refs[-5:]
    part, core = position()
    width = base.shape[1]
    size = width // PARTS // 2
    table = rows[part]
    writes = []
    for n, (s, half, which, index) in enumerate(pieces):
        outer = inverse_rows(table, col, refs[which][index] * (1.0 / replicas))
        start = ((part ^ s) * 2 + (core if half == 0 else 1 - core)) * size
        for g in range(size // GROUP):
            at = slice(GROUP * g, GROUP * (g + 1))
            src = pl.ds(pl.multiple_of(start + GROUP * g, GROUP), GROUP)
            grad = outer[ROWS * g : ROWS * (g + 1)]
            new_momentum = OUTER_BETA * mom[:, src] + grad
            mom_w[n, :, at] = new_momentum
            base_w[n, :, at] = base[:, src] - OUTER_RATE * (grad + OUTER_BETA * new_momentum)
        cols = pl.ds(pl.multiple_of(start, GROUP), size)
        for i, (src, dst) in enumerate(((base_w, base_out), (mom_w, mom_out))):
            writes.append(pltpu.make_async_copy(src.at[n], dst.at[:, cols], sems.at[n, i]))
            writes[-1].start()
    for write in writes:
        write.wait()


def call(kernel, name, inputs, in_specs, out_specs, out_shape, scratch, flops, moved, aliases={}):
    return pl.pallas_call(
        kernel,
        in_specs=in_specs,
        out_specs=out_specs,
        out_shape=out_shape,
        scratch_shapes=scratch,
        compiler_params=pltpu.CompilerParams(vmem_limit_bytes=VMEM_LIMIT),
        cost_estimate=pl.CostEstimate(flops=flops, bytes_accessed=moved, transcendentals=0),
        input_output_aliases=aliases,
        name=name,
    )(*inputs)


def in_hbm(value):
    return pltpu.with_memory_space_constraint(value, pltpu.HBM)


def local(local_params, base_params, error_buffer, momentum):
    rows, width = base_params.shape
    replicas = lax.axis_size("rep")
    shards = lax.axis_size("fsdp")
    quarter_rows = width // PARTS // GROUP * ROWS
    col_fwd, col_inv, rows_fwd, rows_inv = (jnp.asarray(t) for t in tables())
    f32 = lambda *shape: jax.ShapeDtypeStruct(shape, jnp.float32)
    buffer = lambda dtype=jnp.float32: pltpu.VMEM((PARTS, rows, width // PARTS), dtype)
    cells = rows * width

    def forward(*steps):
        count = len(steps)
        pair = lambda dtype=jnp.float32: pltpu.VMEM((count, rows, width // PARTS), dtype)
        coeffs, field = call(
            functools.partial(forward_kernel, steps), "forward",
            [in_hbm(v) for v in (base_params, local_params, error_buffer, col_fwd, rows_fwd)],
            [HBM] * 5,
            [VMEM, VMEM], [pltpu.VMEM((count, 2, quarter_rows // 2, WIDE), jnp.float32), pair()],
            [pair(), pair(jnp.bfloat16), pair(), pltpu.VMEM(col_fwd.shape, jnp.bfloat16), pltpu.VMEM(rows_fwd.shape[1:], jnp.float32),
             pltpu.SemaphoreType.DMA((count, 3)), pltpu.SemaphoreType.DMA((2,))],
            flops=cells * 256 * count, moved=cells * 11 * count // PARTS,
        )
        return tuple(coeffs[i] for i in range(count)), field

    def along_z(value, s, name):
        with jax.named_scope(f"{name}{s}"):
            return lax.ppermute(value, "fsdp", [(i, i ^ s) for i in range(shards)])

    def along_rep(value, s, name):
        with jax.named_scope(f"{name}{s}"):
            return lax.ppermute(value, "rep", [(i, i ^ s) for i in range(replicas)])

    (part3,), field3 = forward(3)
    passed = along_z(part3, 1, "pass")
    (part2, part1, part0), fields = forward(2, 1, 0)
    passed, part1 = lax.optimization_barrier((passed, part1))
    far2 = along_z(part2 + passed, 2, "far")
    near1 = along_z(part1, 1, "near")
    quarter = part0 + far2 + near1
    diag, ylo, beside = along_rep(quarter[1], 3, "diag"), along_rep(quarter[0], 2, "ylo"), along_rep(quarter[1], 1, "core")
    total = quarter[0] + diag + ylo + beside
    x12, x4, x8 = (along_rep(total, s, "x") for s in (12, 4, 8))
    next2, next1 = along_z(quarter, 2, "next"), along_z(quarter, 1, "next")
    next3 = along_z(next2, 1, "relay")
    next1, next2, x8 = lax.optimization_barrier((next1, next2, x8))
    total = total + x8 + x4 + x12
    own_pieces = [total] + [along_z(total, s, "mean") for s in range(1, PARTS)]

    new_error = call(
        error_kernel, "error",
        (quarter, next1, next2, next3, field3, fields, col_inv, rows_inv),
        [VMEM] * 8,
        HBM, f32(1, rows, width),
        [buffer(), pltpu.SemaphoreType.DMA((PARTS,))],
        flops=cells * 1024, moved=cells * 8,
    )
    *own_pieces, new_error = lax.optimization_barrier((*own_pieces, new_error))
    own = jnp.stack(own_pieces)
    other = along_rep(own, 1, "swap")
    batches = (
        ((own,), tuple((s, 0, 0, s) for s in range(PARTS))),
        ((other,), tuple((s, 1, 0, s) for s in range(PARTS))),
    )
    state = ()
    for means, pieces in batches:
        count = len(pieces)
        piece = pltpu.VMEM((count, rows, width // PARTS // 2), jnp.float32)
        state = call(
            functools.partial(update_kernel, replicas, pieces), "update",
            (base_params, momentum, col_inv, rows_inv, *means, *state),
            [VMEM] * (4 + len(means)) + [HBM] * len(state),
            [HBM, HBM], [f32(rows, width), f32(rows, width)],
            [piece, piece, pltpu.SemaphoreType.DMA((count, 2))],
            flops=cells * 128 * count, moved=cells * 2 * count,
            aliases={4 + len(means) + i: i for i in range(len(state))},
        )
    new_base, new_momentum = state
    return (new_base, new_error, new_momentum)


def solution(mesh):
    in_specs = (P("rep", "fsdp", None), P("fsdp", None), P("rep", "fsdp", None), P("fsdp", None))
    out_specs = (P("fsdp", None), P("rep", "fsdp", None), P("fsdp", None))
    return jax.shard_map(local, mesh=mesh, in_specs=in_specs, out_specs=out_specs, check_vma=False)
```

```python
import functools
import math

import jax
import jax.numpy as jnp
import ml_dtypes
import numpy as np
from jax import lax
from jax.experimental import pallas as pl
from jax.experimental.pallas import tpu as pltpu
from jax.sharding import PartitionSpec as P

TILE = 64
BAND = 16
OUTER_RATE = 0.7
OUTER_BETA = 0.9

PARTS = 4
ROWS = TILE // PARTS
GROUP_TILES = 8
GROUP = GROUP_TILES * TILE
WIDE = GROUP_TILES * BAND
VMEM_LIMIT = 24 * 1024 * 1024

HBM = pl.BlockSpec(memory_space=pltpu.HBM)
VMEM = pl.BlockSpec(memory_space=pltpu.VMEM)


def split_np(table):
    high = table.astype(np.float32).astype(ml_dtypes.bfloat16)
    low = (table - high.astype(np.float64)).astype(np.float32).astype(ml_dtypes.bfloat16)
    return high, low


def tables():
    freq = np.arange(BAND, dtype=np.float64)[:, None]
    sample = np.arange(TILE, dtype=np.float64)[None, :]
    scale = np.where(freq == 0, math.sqrt(1.0 / TILE), math.sqrt(2.0 / TILE))
    lowband = scale * np.cos(math.pi * (2.0 * sample + 1.0) * freq / (2.0 * TILE))
    high, low = split_np(np.kron(np.eye(GROUP_TILES), lowband.T))
    col_fwd = np.concatenate([high, low], axis=1)
    col_inv = np.stack([np.concatenate([t.T, t.T], axis=0) for t in (high, low)])
    blocks = [lowband[:, ROWS * part : ROWS * (part + 1)] for part in range(PARTS)]
    rows_fwd = np.stack(blocks).astype(np.float32)
    rows_inv = np.stack([b.T for b in blocks]).astype(np.float32)
    return col_fwd, col_inv, rows_fwd, rows_inv


def split(value):
    high = value.astype(jnp.bfloat16)
    low = (value - high.astype(jnp.float32)).astype(jnp.bfloat16)
    return high, low


def dot(a, b):
    return jnp.dot(a, b, preferred_element_type=jnp.float32)


def apply_rows(table, value):
    deep = value.reshape(-1, table.shape[1], value.shape[1])
    total = None
    for a in range(table.shape[1]):
        term = table[None, :, a : a + 1] * deep[:, a : a + 1, :]
        total = term if total is None else total + term
    return total.reshape(-1, value.shape[1])


def position():
    part = lax.axis_index("fsdp") % PARTS
    core = lax.axis_index("rep") % 2
    return part, core


def quarter_cols(part, s, width):
    size = width // PARTS
    return pl.ds(pl.multiple_of((part ^ s) * size, GROUP), size)


def forward_kernel(steps, base, local, err, col, rows, out, kept, base_v, local_v, err_v, col_v, rows_v, sems, table_sems):
    part, core = position()
    width = base.shape[1]
    tables = (
        pltpu.make_async_copy(col, col_v, table_sems.at[0]),
        pltpu.make_async_copy(rows.at[part], rows_v, table_sems.at[1]),
    )
    copies = []
    for i, s in enumerate(steps):
        cols = quarter_cols(part, s, width)
        copies.append(
            [
                pltpu.make_async_copy(base.at[:, cols], base_v.at[i], sems.at[i, 0]),
                pltpu.make_async_copy(err.at[0, :, cols], err_v.at[i], sems.at[i, 1]),
                pltpu.make_async_copy(local.at[0, :, cols], local_v.at[i], sems.at[i, 2]),
            ]
        )
    for copy in (*copies[0], *tables, *(copy for step in copies[1:] for copy in step)):
        copy.start()
    for copy in (*tables, *(copy for step in copies for copy in step)):
        copy.wait()
    stacked = []
    for i in range(len(steps)):
        for g in range(base_v.shape[2] // GROUP):
            at = slice(GROUP * g, GROUP * (g + 1))
            field = base_v[i, :, at] - local_v[i, :, at].astype(jnp.float32) + err_v[i, :, at]
            kept[i, :, at] = field
            stacked.append(field)
    stacked = jnp.concatenate(stacked, axis=0)
    count = stacked.shape[0]
    both = dot(jnp.concatenate(split(stacked), axis=0), col_v[...])
    both = both[:, :WIDE] + both[:, WIDE:]
    coeffs = apply_rows(rows_v[...], both[:count] + both[count:])
    half = count // len(steps) // 2
    for i in range(len(steps)):
        out[i, core] = coeffs[2 * i * half : (2 * i + 1) * half]
        out[i, 1 - core] = coeffs[(2 * i + 1) * half : (2 * i + 2) * half]


def inverse_rows(table, col, coeffs):
    both = jnp.concatenate(split(apply_rows(table, coeffs)), axis=1)
    return dot(both, col[0]) + dot(both, col[1])


def error_kernel(k0, k1, k2, k3, field3, fields, field0, col, rows, out, out_v, sems):
    part, core = position()
    width = out.shape[2]
    order = ((k0, field0.at[0]), (k1, fields.at[1]), (k2, fields.at[0]), (k3, field3.at[0]))
    coeffs = jnp.concatenate([k[h] for k, _ in order for h in (core, 1 - core)], axis=0)
    kept = inverse_rows(rows[part], col, coeffs)
    count = coeffs.shape[0] // PARTS
    writes = []
    for s, (_, field) in enumerate(order):
        for g in range(count // ROWS):
            row = s * count + ROWS * g
            at = slice(GROUP * g, GROUP * (g + 1))
            out_v[s, :, at] = field[:, at] - kept[row : row + ROWS]
        writes.append(pltpu.make_async_copy(out_v.at[s], out.at[0, :, quarter_cols(part, s, width)], sems.at[s]))
        writes[-1].start()
    for write in writes:
        write.wait()


def update_kernel(replicas, pieces, base, mom, col, rows, *refs):
    base_out, mom_out, base_w, mom_w, sems = refs[-5:]
    part, core = position()
    width = base.shape[1]
    size = width // PARTS // 2
    table = rows[part]
    writes = []
    for n, (s, half, which, index) in enumerate(pieces):
        outer = inverse_rows(table, col, refs[which][index] * (1.0 / replicas))
        start = ((part ^ s) * 2 + (core if half == 0 else 1 - core)) * size
        for g in range(size // GROUP):
            at = slice(GROUP * g, GROUP * (g + 1))
            src = pl.ds(pl.multiple_of(start + GROUP * g, GROUP), GROUP)
            grad = outer[ROWS * g : ROWS * (g + 1)]
            new_momentum = OUTER_BETA * mom[:, src] + grad
            mom_w[n, :, at] = new_momentum
            base_w[n, :, at] = base[:, src] - OUTER_RATE * (grad + OUTER_BETA * new_momentum)
        cols = pl.ds(pl.multiple_of(start, GROUP), size)
        for i, (src, dst) in enumerate(((base_w, base_out), (mom_w, mom_out))):
            writes.append(pltpu.make_async_copy(src.at[n], dst.at[:, cols], sems.at[n, i]))
            writes[-1].start()
    for write in writes:
        write.wait()


def call(kernel, name, inputs, in_specs, out_specs, out_shape, scratch, flops, moved, aliases={}):
    return pl.pallas_call(
        kernel,
        in_specs=in_specs,
        out_specs=out_specs,
        out_shape=out_shape,
        scratch_shapes=scratch,
        compiler_params=pltpu.CompilerParams(vmem_limit_bytes=VMEM_LIMIT),
        cost_estimate=pl.CostEstimate(flops=flops, bytes_accessed=moved, transcendentals=0),
        input_output_aliases=aliases,
        name=name,
    )(*inputs)


def in_hbm(value):
    return pltpu.with_memory_space_constraint(value, pltpu.HBM)


def local(local_params, base_params, error_buffer, momentum):
    rows, width = base_params.shape
    replicas = lax.axis_size("rep")
    shards = lax.axis_size("fsdp")
    quarter_rows = width // PARTS // GROUP * ROWS
    col_fwd, col_inv, rows_fwd, rows_inv = (jnp.asarray(t) for t in tables())
    f32 = lambda *shape: jax.ShapeDtypeStruct(shape, jnp.float32)
    buffer = lambda dtype=jnp.float32: pltpu.VMEM((PARTS, rows, width // PARTS), dtype)
    cells = rows * width

    def forward(*steps):
        count = len(steps)
        pair = lambda dtype=jnp.float32: pltpu.VMEM((count, rows, width // PARTS), dtype)
        coeffs, field = call(
            functools.partial(forward_kernel, steps), "forward",
            [in_hbm(v) for v in (base_params, local_params, error_buffer, col_fwd, rows_fwd)],
            [HBM] * 5,
            [VMEM, VMEM], [pltpu.VMEM((count, 2, quarter_rows // 2, WIDE), jnp.float32), pair()],
            [pair(), pair(jnp.bfloat16), pair(), pltpu.VMEM(col_fwd.shape, jnp.bfloat16), pltpu.VMEM(rows_fwd.shape[1:], jnp.float32),
             pltpu.SemaphoreType.DMA((count, 3)), pltpu.SemaphoreType.DMA((2,))],
            flops=cells * 256 * count, moved=cells * 11 * count // PARTS,
        )
        return tuple(coeffs[i] for i in range(count)), field

    def along_z(value, s, name):
        with jax.named_scope(f"{name}{s}"):
            return lax.ppermute(value, "fsdp", [(i, i ^ s) for i in range(shards)])

    def along_rep(value, s, name):
        with jax.named_scope(f"{name}{s}"):
            return lax.ppermute(value, "rep", [(i, i ^ s) for i in range(replicas)])

    (part3,), field3 = forward(3)
    passed = along_z(part3, 1, "pass")
    (part2, part1), fields = forward(2, 1)
    passed, part1 = lax.optimization_barrier((passed, part1))
    far2 = along_z(part2 + passed, 2, "far")
    near1 = along_z(part1, 1, "near")
    (part0,), field0 = forward(0)
    quarter = part0 + far2 + near1
    diag, ylo, beside = along_rep(quarter[1], 3, "diag"), along_rep(quarter[0], 2, "ylo"), along_rep(quarter[1], 1, "core")
    total = quarter[0] + diag + ylo + beside
    x12, x4, x8 = (along_rep(total, s, "x") for s in (12, 4, 8))
    next2, next1 = along_z(quarter, 2, "next"), along_z(quarter, 1, "next")
    next3 = along_z(next2, 1, "relay")
    next1, next2, x8 = lax.optimization_barrier((next1, next2, x8))
    total = total + x8 + x4 + x12
    own_pieces = [total] + [along_z(total, s, "mean") for s in range(1, PARTS)]

    new_error = call(
        error_kernel, "error",
        (quarter, next1, next2, next3, field3, fields, field0, col_inv, rows_inv),
        [VMEM] * 9,
        HBM, f32(1, rows, width),
        [buffer(), pltpu.SemaphoreType.DMA((PARTS,))],
        flops=cells * 1024, moved=cells * 8,
    )
    *own_pieces, new_error = lax.optimization_barrier((*own_pieces, new_error))
    own = jnp.stack(own_pieces)
    other = along_rep(own, 1, "swap")
    batches = (
        ((own,), tuple((s, 0, 0, s) for s in range(PARTS))),
        ((other,), tuple((s, 1, 0, s) for s in range(PARTS))),
    )
    state = ()
    for means, pieces in batches:
        count = len(pieces)
        piece = pltpu.VMEM((count, rows, width // PARTS // 2), jnp.float32)
        state = call(
            functools.partial(update_kernel, replicas, pieces), "update",
            (base_params, momentum, col_inv, rows_inv, *means, *state),
            [VMEM] * (4 + len(means)) + [HBM] * len(state),
            [HBM, HBM], [f32(rows, width), f32(rows, width)],
            [piece, piece, pltpu.SemaphoreType.DMA((count, 2))],
            flops=cells * 128 * count, moved=cells * 2 * count,
            aliases={4 + len(means) + i: i for i in range(len(state))},
        )
    new_base, new_momentum = state
    return (new_base, new_error, new_momentum)


def solution(mesh):
    in_specs = (P("rep", "fsdp", None), P("fsdp", None), P("rep", "fsdp", None), P("fsdp", None))
    out_specs = (P("fsdp", None), P("rep", "fsdp", None), P("fsdp", None))
    return jax.shard_map(local, mesh=mesh, in_specs=in_specs, out_specs=out_specs, check_vma=False)
```
